32 devices in a mesh: section: 2 (over z_hi), span: 8 (over y, x, core), seq: 2 (over z_lo).
Axes of the slice: x: 2, y: 2, z: 4 (z_hi: 2, z_lo: 2; z = z_hi * 2 + z_lo), core: 2. Of those that a mesh axis runs over, the one named last changes fastest.
Arguments:
- latents: bfloat16 [8064, 5120], P(('span', 'seq')), may hold values from -6 to 6
- queries: bfloat16 [2, 8064, 5120], P('section', ('span', 'seq')), may hold values from -12 to 12, as said below
- key_states: bfloat16 [2, 8064, 5120], P('section', ('span', 'seq')), may hold values from -12 to 12
- value_states: bfloat16 [2, 8064, 5120], P('section', ('span', 'seq')), may hold values from -6 to 6
- gate_scales: float32 [2, 5120], P('section'), may hold values from 4 to 12
- window: int32 [7], replicated, may hold values from 1 to 10, 38 in all
- intersection: int32 [7], replicated, may hold values from 1 to 10, 38 in all
- blend_index: int32 [7, 10], replicated, may hold values from 0 to 7
Outputs:
- denoised: bfloat16 [8064, 5120], P('span', ('section', 'seq'))
The draws below stay inside these ranges and needn't reach their ends.
Inputs may be any that keep to these rules, and one draw needn't show every extreme that they name: `queries`: queries of the span lie in the stated range. `window`: 10 is reached in every draw. `intersection`: 10 is reached in every draw.
All inputs are finite; a program needn't handle non-finite values.
Results may differ from the reference program's by a relative error of at most 0.0095.
Values may be sent and summed in bfloat16 or wider, within the bound.
A program may use at most 192 MiB of HBM per device.

```python
import math
import jax
import jax.numpy as jnp
import numpy as np
from jax import lax

D = 5120
HEADS = 40
HEAD_DIM = 128
FRAMES = 21
TOK_FRAME = 48
BF = 10
WEIGHTS = 8
LAYERS = 2
SPANS = 8
PAIRS = 7
TOKENS = 8064


def draw_queries(key, part):
    base = jnp.clip(1.2 * jax.random.normal(jax.random.fold_in(key, 1), (LAYERS, TOKENS, D), jnp.float32), -12.0, 12.0)
    return base.astype(jnp.bfloat16)


def draw_key_states(key, part):
    base = jnp.clip(1.2 * jax.random.normal(jax.random.fold_in(key, 2), (LAYERS, TOKENS, D), jnp.float32), -12.0, 12.0)
    return base.astype(jnp.bfloat16)


def touch_ends(entries, stream_key, low, largest):
    index_at = [jax.random.randint(jax.random.fold_in(stream_key, axis), (), 0, length) for axis, length in enumerate(entries.shape)]
    widest = entries.shape.index(max(entries.shape))
    beside = index_at[:widest] + [(index_at[widest] + 1) % entries.shape[widest]] + index_at[widest + 1:]
    return entries.at[tuple(index_at)].set(low).at[tuple(beside)].set(largest)


def shard_levels(rng, dims, split, smallest, high):
    def one(dim, blocks):
        draws = jax.random.uniform(jax.random.fold_in(jax.random.fold_in(rng, 6), dim), (blocks,), jnp.float32, smallest / len(split), high / len(split))
        return jnp.repeat(jnp.exp(draws), dims[dim] // blocks).reshape((-1,) + (1,) * (len(dims) - dim - 1))

    loudness = one(*split[0])
    for cut in split[1:]:
        loudness = loudness * one(*cut)
    return loudness


def profile(number_of, total, bound, skew):
    portions = [(1 << 20) // math.isqrt(grade ** skew) + 1 for grade in range(2, number_of + 1)]
    rest, holding = total - bound - (number_of - 1), [1] * (number_of - 1)
    while rest > 0:
        movable = [i for i in range(number_of - 1) if holding[i] < bound]
        whole, left = sum([portions[i] for i in movable]), rest
        for i in movable:
            more = min(bound - holding[i], max(1, left * portions[i] // whole), rest)
            holding[i] = holding[i] + more
            rest = rest - more
    return np.array([bound] + holding)


def uneven(rng, number_of, total, reach, slope):
    if number_of == 2:
        one = jax.random.randint(rng, (), max(1, total - reach), min(reach, total - 1) + 1)
        return jnp.stack([one, total - one])
    sizes = jnp.asarray(profile(number_of, total, reach, slope), jnp.int32)
    twos = (number_of - 1) // 2
    source_of, receiver = sizes[1:1 + 2 * twos:2], sizes[2:2 + 2 * twos:2]
    margin = jnp.minimum(source_of - 1, reach - receiver)
    passed = jax.random.randint(jax.random.fold_in(rng, 1), (twos,), 0, 1 << 20) % (margin + 1)
    sizes = sizes.at[1:1 + 2 * twos:2].set(source_of - passed).at[2:2 + 2 * twos:2].set(receiver + passed)
    return sizes[jax.random.permutation(jax.random.fold_in(rng, 2), number_of)]


def scatter_about(stream_key, dims, scale, reach, pieces=(), kind=jnp.bfloat16):
    entries = scale * jax.random.normal(stream_key, dims, jnp.float32)
    if pieces:
        entries = entries * shard_levels(stream_key, dims, pieces, -0.22, 0.18)
    return jnp.clip(entries, -reach, reach).astype(kind)


def setup_inputs(seed: int = 0) -> dict:
    keys = jax.random.split(jax.random.key(seed), 9)
    return {
        "latents": scatter_about(keys[0], (TOKENS, D), 1.0, 6.0, ((0, 16),)),
        "queries": draw_queries(jax.random.fold_in(keys[8], 71), 0),
        "key_states": draw_key_states(jax.random.fold_in(keys[8], 71), 0),
        "value_states": scatter_about(keys[3], (LAYERS, TOKENS, D), 1.0, 6.0, ((0, 2), (1, 16))),
        "gate_scales": jnp.clip(jnp.exp(math.log(12.0) - 1.0986123 * jax.random.uniform(keys[4], (LAYERS, D), jnp.float32) ** shard_levels(keys[4], (LAYERS, D), ((0, 2),), -0.2, 0.2)), 4.0, 12.0),
        "window": uneven(keys[5], PAIRS, (BF + 1) * PAIRS // 2, BF, 1).astype(jnp.int32),
        "intersection": uneven(keys[6], PAIRS, (BF + 1) * PAIRS // 2, BF, 1).astype(jnp.int32),
        "blend_index": touch_ends(jax.random.randint(keys[7], (PAIRS, BF), 0, WEIGHTS), jax.random.fold_in(keys[7], 1), 0, WEIGHTS - 1).astype(jnp.int32),
    }


def attend_layer(query_all, key_all, value_all, window):
    span_tokens = FRAMES * TOK_FRAME
    tail_rows = BF * TOK_FRAME
    query_spans = query_all.reshape(SPANS, span_tokens, D)
    key_spans = key_all.reshape(SPANS, span_tokens, D)
    value_spans = value_all.reshape(SPANS, span_tokens, D)
    empty = jnp.zeros((1, tail_rows, D), key_all.dtype)
    prev_keys = jnp.concatenate([empty, key_spans[:-1, span_tokens - tail_rows:]], 0)
    prev_values = jnp.concatenate([empty, value_spans[:-1, span_tokens - tail_rows:]], 0)
    reach_all = jnp.concatenate([jnp.zeros((1,), jnp.int32), window.astype(jnp.int32)])

    def per_span(packed):
        query_block, key_block, value_block, key_tail, value_tail, reach_frames = packed
        key_full = jnp.concatenate([key_block, key_tail], 0)
        value_full = jnp.concatenate([value_block, value_tail], 0)
        frame_of = jnp.arange(tail_rows) // TOK_FRAME
        usable = jnp.concatenate([jnp.ones((span_tokens,), bool), frame_of >= BF - reach_frames])
        query_heads = query_block.astype(jnp.float32).reshape(span_tokens, HEADS, HEAD_DIM)
        key_heads = key_full.astype(jnp.float32).reshape(-1, HEADS, HEAD_DIM)
        value_heads = value_full.astype(jnp.float32).reshape(-1, HEADS, HEAD_DIM)
        scores = jnp.einsum('qhd,khd->hqk', query_heads, key_heads) * (1.0 / math.sqrt(HEAD_DIM))
        scores = jnp.where(usable[None, None, :], scores, -jnp.inf)
        row_max = lax.optimization_barrier(jnp.max(scores, axis=-1, keepdims=True))
        lifted = jnp.exp(scores - row_max)
        weights = (lifted / lax.optimization_barrier(jnp.sum(lifted, axis=-1, keepdims=True))).astype(jnp.bfloat16).astype(jnp.float32)
        combined = jnp.einsum('hqk,khd->qhd', weights, value_heads)
        return combined.reshape(span_tokens, D).astype(jnp.bfloat16)
    result = lax.map(per_span, (query_spans, key_spans, value_spans, prev_keys, prev_values, reach_all))
    return result.reshape(TOKENS, D)

def reference(latents, queries, key_states, value_states, gate_scales, window, intersection, blend_index):
    attended_zero = attend_layer(queries[0], key_states[0], value_states[0], window)
    attended_one = attend_layer(queries[1], key_states[1], value_states[1], window)
    after_one = (latents.astype(jnp.float32) + gate_scales[0] * attended_zero.astype(jnp.float32)).astype(jnp.bfloat16)
    second = (after_one.astype(jnp.float32) + gate_scales[1] * attended_one.astype(jnp.float32)).astype(jnp.bfloat16)
    grid = second.reshape(SPANS, FRAMES, TOK_FRAME, D)
    prev_tail = grid[:-1, FRAMES - BF:]
    frame_ids = jnp.arange(BF)
    source = jnp.clip(BF - intersection[:, None] + frame_ids[None, :], 0, BF - 1).astype(jnp.int32)
    picked = jax.vmap(lambda tail_block, picks: jnp.take(tail_block, picks, axis=0))(prev_tail, source)
    picked = picked.astype(jnp.float32)
    weight = ((blend_index.astype(jnp.float32) + 0.5) / WEIGHTS)[:, :, None, None]
    leading = grid[1:, :BF].astype(jnp.float32)
    active = (frame_ids[None, :] < intersection[:, None])[:, :, None, None]
    blended = jnp.where(active, weight * leading + (1.0 - weight) * picked, leading).astype(jnp.bfloat16)
    grid = grid.at[1:, :BF].set(blended)
    return grid.reshape(TOKENS, D)
```

```python
import functools
import math

import jax
import jax.numpy as jnp
from jax import lax
from jax.experimental import pallas as pl
from jax.experimental.pallas import tpu as pltpu
from jax.sharding import PartitionSpec as P

HEAD_DIM = 128
TOK_FRAME = 48
BF = 10
WEIGHTS = 8
SUBS = 2
CHUNKS = 2 * SUBS
MESH = pl.DeviceIdType.MESH


def kernel(
    spans,
    lat_hbm, q_hbm, k_hbm, v_hbm, gate_ref, window_ref,
    second, prev,
    q_buf, k_buf, v_buf, near_k, near_v, att, att_recv, lat, gate_recv, v_ext, k_mask,
    own_sem, lat_sem, seq_send, seq_recv, lat_send, lat_recv, near_send, near_recv,
    sect_send, sect_recv, gate_send, gate_recv_sem, tail_send, tail_recv,
):
    s = lax.axis_index("section")
    c = lax.axis_index("span")
    q = lax.axis_index("seq")
    rows, width = lat_hbm.shape
    quarter = width // 4
    part = quarter // SUBS
    heads = part // HEAD_DIM
    tail_rows = BF * TOK_FRAME
    has_prev = c > 0
    has_next = c < spans - 1
    to_seq = {"seq": 1 - q}
    to_sect = {"section": 1 - s}
    to_next = {"span": jnp.minimum(c + 1, spans - 1)}
    inputs = (k_hbm, v_hbm, q_hbm)
    bufs = (k_buf, v_buf, q_buf)
    nears = (near_k, near_v)

    def columns(j, who):
        t = 1 - s if j < SUBS else s
        return pl.ds(pl.multiple_of((2 * t + who) * quarter + (j % SUBS) * part, 128), part)

    def own_copy(j, i):
        return pltpu.make_async_copy(
            inputs[i].at[0, :, columns(j, q)], bufs[i].at[j, 0], own_sem.at[j, i]
        )

    def seq_copy(j, i):
        return pltpu.make_async_remote_copy(
            src_ref=inputs[i].at[0, :, columns(j, 1 - q)], dst_ref=bufs[i].at[j, 1],
            send_sem=seq_send.at[j, i], recv_sem=seq_recv.at[j, i],
            device_id=to_seq, device_id_type=MESH,
        )

    def near_copy(j, i, straight):
        source = inputs[i].at[0, :, columns(j, q)] if straight else bufs[i].at[j, 1]
        return pltpu.make_async_remote_copy(
            src_ref=source, dst_ref=nears[i].at[j],
            send_sem=near_send.at[j, i], recv_sem=near_recv.at[j, i],
            device_id=to_next, device_id_type=MESH,
        )

    def sect_copy(j):
        return pltpu.make_async_remote_copy(
            src_ref=att.at[j], dst_ref=att_recv.at[j],
            send_sem=sect_send.at[j], recv_sem=sect_recv.at[j],
            device_id=to_sect, device_id_type=MESH,
        )

    def lat_own(jj):
        return pltpu.make_async_copy(
            lat_hbm.at[:, columns(SUBS + jj, q)], lat.at[jj, 0], lat_sem.at[jj]
        )

    def lat_copy(jj):
        return pltpu.make_async_remote_copy(
            src_ref=lat_hbm.at[:, columns(SUBS + jj, 1 - q)], dst_ref=lat.at[jj, 1],
            send_sem=lat_send.at[jj], recv_sem=lat_recv.at[jj],
            device_id=to_seq, device_id_type=MESH,
        )

    gate_copy = pltpu.make_async_remote_copy(
        src_ref=gate_ref, dst_ref=gate_recv, send_sem=gate_send.at[0],
        recv_sem=gate_recv_sem.at[0], device_id=to_sect, device_id_type=MESH,
    )

    def tail_copy(jj):
        piece = pl.ds(jj * part, part)
        return pltpu.make_async_remote_copy(
            src_ref=second.at[1, :, piece], dst_ref=prev.at[:, piece],
            send_sem=tail_send.at[jj], recv_sem=tail_recv.at[jj],
            device_id=to_next, device_id_type=MESH,
        )

    barrier = pltpu.get_barrier_semaphore()
    pl.semaphore_signal(barrier, inc=1, device_id=to_seq, device_id_type=MESH)
    pl.semaphore_signal(barrier, inc=1, device_id=to_sect, device_id_type=MESH)

    @pl.when(has_next)
    def _():
        pl.semaphore_signal(barrier, inc=1, device_id=to_next, device_id_type=MESH)

    @pl.when(has_prev)
    def _():
        pl.semaphore_signal(
            barrier, inc=1, device_id={"span": jnp.maximum(c - 1, 0)}, device_id_type=MESH
        )

    neighbours = 2 + jnp.where(has_next, 1, 0) + jnp.where(has_prev, 1, 0)
    pl.semaphore_wait(barrier, neighbours)

    for i in range(3):
        seq_copy(0, i).start()

    def straight_near(j):
        @pl.when(has_next & (q == 1))
        def _():
            for i in range(2):
                near_copy(j, i, True).start()

    straight_near(0)
    gate_copy.start()
    for j in range(CHUNKS):
        for i in range(3):
            own_copy(j, i).start()
    for jj in range(SUBS):
        lat_own(jj).start()

    reach = jnp.where(has_prev, window_ref[jnp.maximum(c - 1, 0)], 0)
    first_open = rows - reach * TOK_FRAME
    open_rows = lax.broadcasted_iota(jnp.int32, (rows, HEAD_DIM), 0) >= first_open
    ones = jnp.ones((rows, HEAD_DIM), jnp.bfloat16)
    v_ext[0, :, HEAD_DIM:] = ones
    v_ext[1, :, HEAD_DIM:] = ones
    v_ext[2, :, HEAD_DIM:] = jnp.where(open_rows, 1.0, 0.0).astype(jnp.bfloat16)

    @pl.when(jnp.logical_not(has_prev))
    def _():
        near_k[...] = jnp.zeros_like(near_k)
        near_v[...] = jnp.zeros_like(near_v)
        prev[...] = jnp.zeros_like(prev)

    factor = math.log2(math.e) / math.sqrt(HEAD_DIM)

    def attend(j):
        def one_head(head, carry):
            lanes = pl.ds(pl.multiple_of(head * HEAD_DIM, HEAD_DIM), HEAD_DIM)
            open_now = lax.broadcasted_iota(jnp.int32, (rows, HEAD_DIM), 0) >= first_open
            key_own = k_buf[j, 0, :, lanes]
            spare = key_own[:8].astype(jnp.float32)[:1]
            k_mask[...] = jnp.where(
                open_now, near_k[j, :, lanes].astype(jnp.float32), spare
            ).astype(jnp.bfloat16)
            v_ext[0, :, :HEAD_DIM] = v_buf[j, 0, :, lanes]
            v_ext[1, :, :HEAD_DIM] = v_buf[j, 1, :, lanes]
            v_ext[2, :, :HEAD_DIM] = jnp.where(
                open_now, near_v[j, :, lanes].astype(jnp.float32), 0.0
            ).astype(jnp.bfloat16)

            def one_side(who, carry):
                query = q_buf[j, who, :, lanes]
                keys = (k_buf[j, 0, :, lanes], k_buf[j, 1, :, lanes], k_mask[...])
                scores = [
                    lax.dot_general(
                        query, key, (((1,), (1,)), ((), ())), preferred_element_type=jnp.float32
                    )
                    for key in keys
                ]
                top = functools.reduce(
                    jnp.maximum, [jnp.max(x, axis=-1, keepdims=True) for x in scores]
                )
                total = None
                for n, x in enumerate(scores):
                    lifted = jnp.exp2((x - top) * factor).astype(jnp.bfloat16)
                    term = jnp.dot(lifted, v_ext[n], preferred_element_type=jnp.float32)
                    total = term if total is None else total + term
                result = total[:, :HEAD_DIM] / total[:, HEAD_DIM:]
                att[j, lax.rem(who + q, 2), :, lanes] = result.astype(jnp.bfloat16)
                return carry

            return lax.fori_loop(0, 2, one_side, carry)

        lax.fori_loop(0, heads, one_head, 0)

    for j in range(CHUNKS):
        for i in range(3):
            seq_copy(j, i).wait_recv()
            if j + 1 < CHUNKS:
                seq_copy(j + 1, i).start()
            if i < 2:
                @pl.when(has_next & (q == 0))
                def _():
                    near_copy(j, i, False).start()
        if j + 1 < CHUNKS:
            straight_near(j + 1)
        if j >= SUBS:
            lat_copy(j - SUBS).start()
        for i in range(3):
            own_copy(j, i).wait()

        @pl.when(has_prev)
        def _():
            for i in range(2):
                near_copy(j, i, False).wait_recv()

        attend(j)
        if j < SUBS:
            sect_copy(j).start()

    gate_copy.wait_recv()
    for jj in range(SUBS):
        lat_own(jj).wait()
        lat_copy(jj).wait_recv()
        sect_copy(jj).wait_recv()

        def finish(block, carry):
            side, lane_block = lax.rem(block, 2), block // 2
            at = pl.multiple_of(lane_block * HEAD_DIM, HEAD_DIM)
            lanes = pl.ds(at, HEAD_DIM)
            place = pl.ds(
                pl.multiple_of((2 * s + q) * quarter + jj * part + at, HEAD_DIM), HEAD_DIM
            )
            gate_own, gate_other = gate_ref[:, place], gate_recv[:, place]
            mine = att[SUBS + jj, side, :, lanes].astype(jnp.float32)
            other = att_recv[jj, side, :, lanes].astype(jnp.float32)
            gated_own, gated_other = gate_own * mine, gate_other * other
            first = jnp.where(s == 0, gated_own, gated_other)
            later = jnp.where(s == 0, gated_other, gated_own)
            base = lat[jj, lax.rem(side + q, 2), :, lanes].astype(jnp.float32)
            after_one = (base + first).astype(jnp.bfloat16)
            result = (after_one.astype(jnp.float32) + later).astype(jnp.bfloat16)
            second[side, :, pl.ds(pl.multiple_of(jj * part + at, HEAD_DIM), HEAD_DIM)] = result
            return carry

        lax.fori_loop(0, 2 * heads, finish, 0)

        @pl.when(has_next)
        def _():
            tail_copy(jj).start()

    for jj in range(SUBS):
        @pl.when(has_prev)
        def _():
            tail_copy(jj).wait_recv()

        @pl.when(has_next)
        def _():
            tail_copy(jj).wait_send()

        sect_copy(jj).wait_send()
        lat_copy(jj).wait_send()
    gate_copy.wait_send()
    for j in range(CHUNKS):
        for i in range(3):
            seq_copy(j, i).wait_send()

        @pl.when(has_next)
        def _():
            for i in range(2):
                near_copy(j, i, False).wait_send()


def local(
    latents, queries, key_states, value_states, gate_scales, window, intersection, blend_index
):
    rows, width = latents.shape
    quarter = width // 4
    part = quarter // SUBS
    spans = lax.axis_size("span")
    span_pos = lax.axis_index("span")
    tail_rows = BF * TOK_FRAME
    wide = jnp.bfloat16
    dma = pltpu.SemaphoreType.DMA
    flops = 4 * 2 * rows * 3 * rows * width // 2
    second, prev = pl.pallas_call(
        functools.partial(kernel, spans),
        out_shape=(
            jax.ShapeDtypeStruct((2, rows, quarter), wide),
            jax.ShapeDtypeStruct((rows, quarter), wide),
        ),
        in_specs=[pl.BlockSpec(memory_space=pl.ANY)] * 4
        + [pl.BlockSpec(memory_space=pltpu.VMEM), pl.BlockSpec(memory_space=pltpu.SMEM)],
        out_specs=(pl.BlockSpec(memory_space=pltpu.VMEM),) * 2,
        scratch_shapes=[
            pltpu.VMEM((CHUNKS, 2, rows, part), wide),
            pltpu.VMEM((CHUNKS, 2, rows, part), wide),
            pltpu.VMEM((CHUNKS, 2, rows, part), wide),
            pltpu.VMEM((CHUNKS, rows, part), wide),
            pltpu.VMEM((CHUNKS, rows, part), wide),
            pltpu.VMEM((CHUNKS, 2, rows, part), wide),
            pltpu.VMEM((SUBS, 2, rows, part), wide),
            pltpu.VMEM((SUBS, 2, rows, part), wide),
            pltpu.VMEM(gate_scales.shape, jnp.float32),
            pltpu.VMEM((3, rows, 2 * HEAD_DIM), wide),
            pltpu.VMEM((rows, HEAD_DIM), wide),
            dma((CHUNKS, 3)), dma((SUBS,)), dma((CHUNKS, 3)), dma((CHUNKS, 3)),
            dma((SUBS,)), dma((SUBS,)), dma((CHUNKS, 2)), dma((CHUNKS, 2)),
            dma((SUBS,)), dma((SUBS,)), dma((1,)), dma((1,)), dma((SUBS,)), dma((SUBS,)),
        ],
        cost_estimate=pl.CostEstimate(
            flops=flops, bytes_accessed=8 * rows * width, transcendentals=flops // 512
        ),
        compiler_params=pltpu.CompilerParams(
            collective_id=0, has_side_effects=True, vmem_limit_bytes=60 * 1024 * 1024
        ),
    )(latents, queries, key_states, value_states, gate_scales, window)

    earlier = jnp.maximum(span_pos - 1, 0)
    whole = second.reshape(2 * rows, quarter)
    previous = prev[rows - tail_rows:].reshape(BF, TOK_FRAME, quarter)
    length = intersection[earlier]
    frame_ids = jnp.arange(BF)
    source = jnp.clip(BF - length + frame_ids, 0, BF - 1)
    picked = jnp.take(previous, source, axis=0).astype(jnp.float32)
    weight = ((blend_index[earlier].astype(jnp.float32) + 0.5) / WEIGHTS)[:, None, None]
    active = (frame_ids < length) & (span_pos > 0)
    leading = whole[:tail_rows].reshape(BF, TOK_FRAME, quarter).astype(jnp.float32)
    blended = jnp.where(active[:, None, None], weight * leading + (1.0 - weight) * picked, leading)
    blended = blended.astype(wide).reshape(tail_rows, quarter)
    return jnp.concatenate([blended, whole[tail_rows:]], 0)


def solution(mesh):
    in_specs = (
        P(("span", "seq"), None),
        P("section", ("span", "seq"), None),
        P("section", ("span", "seq"), None),
        P("section", ("span", "seq"), None),
        P("section", None),
        P(),
        P(),
        P(),
    )
    out_specs = P("span", ("section", "seq"))
    return jax.shard_map(local, mesh=mesh, in_specs=in_specs, out_specs=out_specs, check_vma=False)
```

```python
import functools
import math

import jax
import jax.numpy as jnp
from jax import lax
from jax.experimental import pallas as pl
from jax.experimental.pallas import tpu as pltpu
from jax.sharding import PartitionSpec as P

HEAD_DIM = 128
TOK_FRAME = 48
BF = 10
WEIGHTS = 8
SLOTS = 6
SHARED = 2
LAST = SLOTS - 1
MESH = pl.DeviceIdType.MESH


def kernel(
    spans,
    lat_hbm, q_hbm, k_hbm, v_hbm, gate_ref, window_ref,
    second, prev,
    q_buf, k_buf, v_buf, near_k, near_v, att_far, att_own, att_recv, lat, tail,
    gate_recv, v_ext, k_mask,
    own_sem, lat_sem, seq_send, seq_recv, lat_send, lat_recv, near_send, near_recv,
    sect_send, sect_recv, gate_send, gate_recv_sem, tail_send, tail_recv,
):
    s = lax.axis_index("section")
    c = lax.axis_index("span")
    q = lax.axis_index("seq")
    rows, width = lat_hbm.shape
    quarter = width // 4
    part = q_buf.shape[3]
    rest = quarter - 2 * part
    tail_rows = BF * TOK_FRAME
    has_prev = c > 0
    has_next = c < spans - 1
    inner = q != s
    outer = q == s
    to_seq = {"seq": 1 - q}
    to_sect = {"section": 1 - s}
    to_cross = {"section": 1 - s, "seq": 1 - q}
    to_next = {"span": jnp.minimum(c + 1, spans - 1)}
    inputs = (k_hbm, v_hbm, q_hbm)
    bufs = (k_buf, v_buf, q_buf)
    nears = (near_k, near_v)

    def breadth(n):
        return rest if n == LAST else part

    def columns(n, who):
        if n < SHARED:
            first = (1 - s) * 2 * quarter + who * (quarter + rest) + n * part
        elif n == SHARED:
            first = (1 - s) * 2 * quarter + 2 * part
        else:
            first = (2 * s + who) * quarter + (n - 3) * part
        return pl.ds(pl.multiple_of(first, HEAD_DIM), breadth(n))

    def place(ref, n, who):
        return ref.at[n, who, :, pl.ds(0, breadth(n))]

    def own_copy(n, i):
        return pltpu.make_async_copy(
            inputs[i].at[0, :, columns(n, q)], place(bufs[i], n, 0), own_sem.at[n, i]
        )

    def seq_copy(n, i):
        return pltpu.make_async_remote_copy(
            src_ref=inputs[i].at[0, :, columns(n, 1 - q)], dst_ref=place(bufs[i], n, 1),
            send_sem=seq_send.at[n, i], recv_sem=seq_recv.at[n, i],
            device_id=to_seq, device_id_type=MESH,
        )

    def near_copy(n, i, straight):
        source = inputs[i].at[0, :, columns(n, q)] if straight else place(bufs[i], n, 1)
        return pltpu.make_async_remote_copy(
            src_ref=source, dst_ref=nears[i].at[n, :, pl.ds(0, breadth(n))],
            send_sem=near_send.at[n, i], recv_sem=near_recv.at[n, i],
            device_id=to_next, device_id_type=MESH,
        )

    def sect_copy(n):
        at = pl.multiple_of(q * rest + n * part, HEAD_DIM)
        return pltpu.make_async_remote_copy(
            src_ref=att_far.at[n], dst_ref=att_recv.at[:, :, pl.ds(at, part)],
            send_sem=sect_send.at[n], recv_sem=sect_recv.at[n],
            device_id=to_sect, device_id_type=MESH,
        )

    def shared_copy(cross):
        whose = 1 - q if cross else q
        source = pl.ds(pl.multiple_of(whose * rest, HEAD_DIM), rest)
        target = pl.ds(pl.multiple_of((1 - whose) * 2 * part, HEAD_DIM), rest)
        return pltpu.make_async_remote_copy(
            src_ref=att_far.at[SHARED, :, :, source], dst_ref=att_recv.at[:, :, target],
            send_sem=sect_send.at[SHARED + cross], recv_sem=sect_recv.at[SHARED],
            device_id=to_cross if cross else to_sect, device_id_type=MESH,
        )

    lat_own = pltpu.make_async_copy(
        lat_hbm.at[:, pl.ds(pl.multiple_of((2 * s + q) * quarter, HEAD_DIM), quarter)],
        lat.at[0], lat_sem.at[0],
    )

    def lat_copy(cross):
        section = 1 - s if cross else s
        source = pl.ds(pl.multiple_of((2 * section + 1 - q) * quarter, HEAD_DIM), quarter)
        return pltpu.make_async_remote_copy(
            src_ref=lat_hbm.at[:, source], dst_ref=lat.at[1],
            send_sem=lat_send.at[cross], recv_sem=lat_recv.at[0],
            device_id=to_cross if cross else to_seq, device_id_type=MESH,
        )

    gate_copy = pltpu.make_async_remote_copy(
        src_ref=gate_ref, dst_ref=gate_recv, send_sem=gate_send.at[0],
        recv_sem=gate_recv_sem.at[0], device_id=to_sect, device_id_type=MESH,
    )
    pieces = ((0, 2 * part), (2 * part, rest))

    def tail_copy(jj):
        piece = pl.ds(*pieces[jj])
        return pltpu.make_async_remote_copy(
            src_ref=tail.at[:, piece], dst_ref=prev.at[:, piece],
            send_sem=tail_send.at[jj], recv_sem=tail_recv.at[jj],
            device_id=to_next, device_id_type=MESH,
        )

    barrier = pltpu.get_barrier_semaphore()
    pl.semaphore_signal(barrier, inc=1, device_id=to_seq, device_id_type=MESH)
    pl.semaphore_signal(barrier, inc=1, device_id=to_sect, device_id_type=MESH)

    @pl.when(inner)
    def _():
        pl.semaphore_signal(barrier, inc=1, device_id=to_cross, device_id_type=MESH)

    @pl.when(has_next)
    def _():
        pl.semaphore_signal(barrier, inc=1, device_id=to_next, device_id_type=MESH)

    @pl.when(has_prev)
    def _():
        pl.semaphore_signal(
            barrier, inc=1, device_id={"span": jnp.maximum(c - 1, 0)}, device_id_type=MESH
        )

    neighbours = 2 + sum(jnp.where(x, 1, 0) for x in (inner, has_next, has_prev))
    pl.semaphore_wait(barrier, neighbours)

    def takes_part(n, cond):
        return cond & inner if n == SHARED else cond

    def straight_near(n):
        @pl.when(takes_part(n, has_next & (q == 1)))
        def _():
            for i in range(2):
                near_copy(n, i, True).start()

    def start_seq(n, i):
        if n == SHARED:
            @pl.when(outer)
            def _():
                seq_copy(n, i).start()

            if i == 0:
                @pl.when(inner)
                def _():
                    lat_copy(0).start()
        elif n < SLOTS:
            seq_copy(n, i).start()

    def start_own(n):
        for i in range(3):
            own_copy(n, i).start()

    for i in range(3):
        start_seq(0, i)
    straight_near(0)
    gate_copy.start()
    for n in range(SLOTS):
        if n == SHARED:
            @pl.when(inner)
            def _():
                start_own(SHARED)
                lat_copy(1).start()
        else:
            start_own(n)
    lat_own.start()

    earlier = jnp.maximum(c - 1, 0)
    reach = jnp.where(has_prev, window_ref[earlier], 0)
    first_open = rows - reach * TOK_FRAME
    open_rows = lax.broadcasted_iota(jnp.int32, (rows, HEAD_DIM), 0) >= first_open
    ones = jnp.ones((rows, HEAD_DIM), jnp.bfloat16)
    v_ext[0, :, HEAD_DIM:] = ones
    v_ext[1, :, HEAD_DIM:] = ones
    v_ext[2, :, HEAD_DIM:] = jnp.where(open_rows, 1.0, 0.0).astype(jnp.bfloat16)

    @pl.when(jnp.logical_not(has_prev))
    def _():
        near_k[...] = jnp.zeros_like(near_k)
        near_v[...] = jnp.zeros_like(near_v)
        prev[...] = jnp.zeros_like(prev)

    factor = math.log2(math.e) / math.sqrt(HEAD_DIM)

    def attend(n):
        def one_head(head, carry):
            at = pl.multiple_of(head * HEAD_DIM, HEAD_DIM)
            lanes = pl.ds(at, HEAD_DIM)
            open_now = lax.broadcasted_iota(jnp.int32, (rows, HEAD_DIM), 0) >= first_open
            spare = k_buf[n, 0, :, lanes][:8].astype(jnp.float32)[:1]
            k_mask[...] = jnp.where(
                open_now, near_k[n, :, lanes].astype(jnp.float32), spare
            ).astype(jnp.bfloat16)
            v_ext[0, :, :HEAD_DIM] = v_buf[n, 0, :, lanes]
            v_ext[1, :, :HEAD_DIM] = v_buf[n, 1, :, lanes]
            v_ext[2, :, :HEAD_DIM] = jnp.where(
                open_now, near_v[n, :, lanes].astype(jnp.float32), 0.0
            ).astype(jnp.bfloat16)

            def one_side(who, carry):
                query = q_buf[n, who, :, lanes]
                keys = (k_buf[n, 0, :, lanes], k_buf[n, 1, :, lanes], k_mask[...])
                scores = [
                    lax.dot_general(
                        query, key, (((1,), (1,)), ((), ())), preferred_element_type=jnp.float32
                    )
                    for key in keys
                ]
                top = functools.reduce(
                    jnp.maximum, [jnp.max(x, axis=-1, keepdims=True) for x in scores]
                )
                total = None
                for m, x in enumerate(scores):
                    lifted = jnp.exp2((x - top) * factor).astype(jnp.bfloat16)
                    term = jnp.dot(lifted, v_ext[m], preferred_element_type=jnp.float32)
                    total = term if total is None else total + term
                result = (total[:, :HEAD_DIM] / total[:, HEAD_DIM:]).astype(jnp.bfloat16)
                side = lax.rem(who + q, 2)
                if n <= SHARED:
                    att_far[n, side, :, lanes] = result
                else:
                    here = pl.multiple_of((n - 3) * part + at, HEAD_DIM)
                    att_own[side, :, pl.ds(here, HEAD_DIM)] = result
                return carry

            return lax.fori_loop(0, 2, one_side, carry)

        lax.fori_loop(0, breadth(n) // HEAD_DIM, one_head, 0)

    def finish(jj):
        def block(step, carry):
            at = pl.multiple_of(pieces[jj][0] + step * HEAD_DIM, HEAD_DIM)
            lanes = pl.ds(at, HEAD_DIM)
            spot = pl.ds(pl.multiple_of((2 * s + q) * quarter + at, HEAD_DIM), HEAD_DIM)
            gate_own, gate_other = gate_ref[:, spot], gate_recv[:, spot]
            for side in range(2):
                gated_own = gate_own * att_own[side, :, lanes].astype(jnp.float32)
                gated_other = gate_other * att_recv[side, :, lanes].astype(jnp.float32)
                first = jnp.where(s == 0, gated_own, gated_other)
                later = jnp.where(s == 0, gated_other, gated_own)
                base = lat[lax.rem(side + q, 2), :, lanes].astype(jnp.float32)
                after_one = (base + first).astype(jnp.bfloat16)
                result = after_one.astype(jnp.float32) + later
                second[side, :, lanes] = result.astype(jnp.bfloat16)
                if side == 1:
                    tail[:, lanes] = result[rows - tail_rows:].astype(jnp.bfloat16)
            return carry

        lax.fori_loop(0, pieces[jj][1] // HEAD_DIM, block, 0)

        @pl.when(has_next)
        def _():
            tail_copy(jj).start()

    def ready(n):
        for i in range(3):
            own_copy(n, i).wait()

        @pl.when(has_prev)
        def _():
            for i in range(2):
                near_copy(n, i, False).wait_recv()

        attend(n)

    for n in range(SLOTS):
        for i in range(3):
            if n == SHARED:
                @pl.when(inner)
                def _():
                    seq_copy(n, i).wait_recv()

                @pl.when(outer)
                def _():
                    seq_copy(n, i).wait_send()
            else:
                seq_copy(n, i).wait_recv()
            start_seq(n + 1, i)
            if i < 2:
                @pl.when(takes_part(n, has_next & (q == 0)))
                def _():
                    near_copy(n, i, False).start()
        if n < LAST:
            straight_near(n + 1)
        if n == SHARED:
            @pl.when(inner)
            def _():
                ready(SHARED)
                for cross in range(2):
                    shared_copy(cross).start()
        else:
            ready(n)
        if n < SHARED:
            sect_copy(n).start()
        if n == LAST - 1:
            gate_copy.wait_recv()
            lat_own.wait()
            lat_copy(0).wait_recv()
            for m in range(SHARED):
                sect_copy(m).wait_recv()
            shared_copy(0).wait_recv()
            finish(0)
    finish(1)
    for jj in range(2):
        @pl.when(has_prev)
        def _():
            tail_copy(jj).wait_recv()

    @pl.when(inner)
    def _():
        for cross in range(2):
            shared_copy(cross).wait_send()
            lat_copy(cross).wait_send()

    for n in range(SHARED):
        sect_copy(n).wait_send()
    gate_copy.wait_send()
    for n in range(SLOTS):
        if n != SHARED:
            for i in range(3):
                seq_copy(n, i).wait_send()

        @pl.when(takes_part(n, has_next))
        def _():
            for i in range(2):
                near_copy(n, i, False).wait_send()

    @pl.when(has_next)
    def _():
        for jj in range(2):
            tail_copy(jj).wait_send()


def blend_kernel(second, prev, inter_ref, blend_ref, out):
    c = lax.axis_index("span")
    earlier = jnp.maximum(c - 1, 0)
    length = jnp.where(c > 0, inter_ref[earlier], 0)
    out[...] = second[...]

    def frame(f, carry):
        source = pl.ds(pl.multiple_of((BF - length + f) * TOK_FRAME, 16), TOK_FRAME)
        here = pl.ds(pl.multiple_of(f * TOK_FRAME, 16), TOK_FRAME)
        weight = (blend_ref[earlier, f].astype(jnp.float32) + 0.5) / WEIGHTS
        leading = second[0, here, :].astype(jnp.float32)
        mixed = weight * leading + (1.0 - weight) * prev[source, :].astype(jnp.float32)
        out[0, here, :] = mixed.astype(jnp.bfloat16)
        return carry

    lax.fori_loop(0, length, frame, 0)


def local(
    latents, queries, key_states, value_states, gate_scales, window, intersection, blend_index
):
    rows, width = latents.shape
    quarter = width // 4
    part = quarter // HEAD_DIM * 2 // 5 * HEAD_DIM
    spans = lax.axis_size("span")
    tail_rows = BF * TOK_FRAME
    wide = jnp.bfloat16
    dma = pltpu.SemaphoreType.DMA
    flops = 4 * 2 * rows * 3 * rows * width // 2
    smem = pl.BlockSpec(memory_space=pltpu.SMEM)
    vmem = pl.BlockSpec(memory_space=pltpu.VMEM)
    second, prev = pl.pallas_call(
        functools.partial(kernel, spans),
        out_shape=(
            jax.ShapeDtypeStruct((2, rows, quarter), wide),
            jax.ShapeDtypeStruct((tail_rows, quarter), wide),
        ),
        in_specs=[pl.BlockSpec(memory_space=pl.ANY)] * 4 + [vmem, smem],
        out_specs=(vmem, vmem),
        scratch_shapes=[
            pltpu.VMEM((SLOTS, 2, rows, part), wide),
            pltpu.VMEM((SLOTS, 2, rows, part), wide),
            pltpu.VMEM((SLOTS, 2, rows, part), wide),
            pltpu.VMEM((SLOTS, rows, part), wide),
            pltpu.VMEM((SLOTS, rows, part), wide),
            pltpu.VMEM((SHARED + 1, 2, rows, part), wide),
            pltpu.VMEM((2, rows, quarter), wide),
            pltpu.VMEM((2, rows, quarter), wide),
            pltpu.VMEM((2, rows, quarter), wide),
            pltpu.VMEM((tail_rows, quarter), wide),
            pltpu.VMEM(gate_scales.shape, jnp.float32),
            pltpu.VMEM((3, rows, 2 * HEAD_DIM), wide),
            pltpu.VMEM((rows, HEAD_DIM), wide),
            dma((SLOTS, 3)), dma((1,)), dma((SLOTS, 3)), dma((SLOTS, 3)),
            dma((2,)), dma((1,)), dma((SLOTS, 2)), dma((SLOTS, 2)),
            dma((SHARED + 2,)), dma((SHARED + 1,)), dma((1,)), dma((1,)), dma((2,)), dma((2,)),
        ],
        cost_estimate=pl.CostEstimate(
            flops=flops, bytes_accessed=8 * rows * width, transcendentals=flops // 512
        ),
        compiler_params=pltpu.CompilerParams(
            collective_id=0, has_side_effects=True, vmem_limit_bytes=60 * 1024 * 1024
        ),
    )(latents, queries, key_states, value_states, gate_scales, window)
    block = 2 * HEAD_DIM
    result = pl.pallas_call(
        blend_kernel,
        grid=(quarter // block,),
        out_shape=jax.ShapeDtypeStruct((2, rows, quarter), wide),
        in_specs=[
            pl.BlockSpec((2, rows, block), lambda i: (0, 0, i)),
            pl.BlockSpec((tail_rows, block), lambda i: (0, i)),
            smem,
            smem,
        ],
        out_specs=pl.BlockSpec((2, rows, block), lambda i: (0, 0, i)),
        compiler_params=pltpu.CompilerParams(vmem_limit_bytes=16 * 1024 * 1024),
    )(second, prev, intersection, blend_index)
    return result.reshape(2 * rows, quarter)


def solution(mesh):
    in_specs = (
        P(("span", "seq"), None),
        P("section", ("span", "seq"), None),
        P("section", ("span", "seq"), None),
        P("section", ("span", "seq"), None),
        P("section", None),
        P(),
        P(),
        P(),
    )
    out_specs = P("span", ("section", "seq"))
    return jax.shard_map(local, mesh=mesh, in_specs=in_specs, out_specs=out_specs, check_vma=False)
```

```python
import functools
import math

import jax
import jax.numpy as jnp
from jax import lax
from jax.experimental import pallas as pl
from jax.experimental.pallas import tpu as pltpu
from jax.sharding import PartitionSpec as P

HEAD_DIM = 128
TOK_FRAME = 48
BF = 10
WEIGHTS = 8
SLOTS = 6
SHARED = 2
LAST = SLOTS - 1
IN_FLIGHT = 5
MESH = pl.DeviceIdType.MESH


def kernel(
    spans,
    lat_hbm, q_hbm, k_hbm, v_hbm, gate_ref, window_ref,
    second, prev,
    q_buf, k_buf, v_buf, near_k, near_v, att_far, att_own, att_recv, lat, tail,
    gate_recv, v_ext, k_mask,
    own_sem, lat_sem, seq_send, seq_recv, lat_send, lat_recv, near_send, near_recv,
    sect_send, sect_recv, gate_send, gate_recv_sem, tail_send, tail_recv,
):
    s = lax.axis_index("section")
    c = lax.axis_index("span")
    q = lax.axis_index("seq")
    rows, width = lat_hbm.shape
    quarter = width // 4
    part = q_buf.shape[3]
    rest = quarter - 2 * part
    tail_rows = BF * TOK_FRAME
    has_prev = c > 0
    has_next = c < spans - 1
    inner = q != s
    outer = q == s
    to_seq = {"seq": 1 - q}
    to_sect = {"section": 1 - s}
    to_cross = {"section": 1 - s, "seq": 1 - q}
    to_next = {"span": jnp.minimum(c + 1, spans - 1)}
    inputs = (k_hbm, v_hbm, q_hbm)
    bufs = (k_buf, v_buf, q_buf)
    nears = (near_k, near_v)

    def breadth(n):
        return rest if n == LAST else part

    def columns(n, who):
        if n < SHARED:
            first = (1 - s) * 2 * quarter + who * (quarter + rest) + n * part
        elif n == SHARED:
            first = (1 - s) * 2 * quarter + 2 * part
        else:
            first = (2 * s + who) * quarter + (n - 3) * part
        return pl.ds(pl.multiple_of(first, HEAD_DIM), breadth(n))

    def place(ref, n, who):
        return ref.at[n, who, :, pl.ds(0, breadth(n))]

    def own_copy(n, i):
        return pltpu.make_async_copy(
            inputs[i].at[0, :, columns(n, q)], place(bufs[i], n, 0), own_sem.at[n, i]
        )

    def seq_copy(n, i):
        return pltpu.make_async_remote_copy(
            src_ref=inputs[i].at[0, :, columns(n, 1 - q)], dst_ref=place(bufs[i], n, 1),
            send_sem=seq_send.at[n, i], recv_sem=seq_recv.at[n, i],
            device_id=to_seq, device_id_type=MESH,
        )

    def near_copy(n, i, straight):
        source = inputs[i].at[0, :, columns(n, q)] if straight else place(bufs[i], n, 1)
        return pltpu.make_async_remote_copy(
            src_ref=source, dst_ref=nears[i].at[n, :, pl.ds(0, breadth(n))],
            send_sem=near_send.at[n, i], recv_sem=near_recv.at[n, i],
            device_id=to_next, device_id_type=MESH,
        )

    def sect_copy(n):
        at = pl.multiple_of(q * rest + n * part, HEAD_DIM)
        return pltpu.make_async_remote_copy(
            src_ref=att_far.at[n], dst_ref=att_recv.at[:, :, pl.ds(at, part)],
            send_sem=sect_send.at[n], recv_sem=sect_recv.at[n],
            device_id=to_sect, device_id_type=MESH,
        )

    def shared_copy(cross):
        whose = 1 - q if cross else q
        source = pl.ds(pl.multiple_of(whose * rest, HEAD_DIM), rest)
        target = pl.ds(pl.multiple_of((1 - whose) * 2 * part, HEAD_DIM), rest)
        return pltpu.make_async_remote_copy(
            src_ref=att_far.at[SHARED, :, :, source], dst_ref=att_recv.at[:, :, target],
            send_sem=sect_send.at[SHARED + cross], recv_sem=sect_recv.at[SHARED],
            device_id=to_cross if cross else to_sect, device_id_type=MESH,
        )

    lat_own = pltpu.make_async_copy(
        lat_hbm.at[:, pl.ds(pl.multiple_of((2 * s + q) * quarter, HEAD_DIM), quarter)],
        lat.at[0], lat_sem.at[0],
    )

    def lat_copy(cross):
        section = 1 - s if cross else s
        source = pl.ds(pl.multiple_of((2 * section + 1 - q) * quarter, HEAD_DIM), quarter)
        return pltpu.make_async_remote_copy(
            src_ref=lat_hbm.at[:, source], dst_ref=lat.at[1],
            send_sem=lat_send.at[cross], recv_sem=lat_recv.at[0],
            device_id=to_cross if cross else to_seq, device_id_type=MESH,
        )

    gate_copy = pltpu.make_async_remote_copy(
        src_ref=gate_ref, dst_ref=gate_recv, send_sem=gate_send.at[0],
        recv_sem=gate_recv_sem.at[0], device_id=to_sect, device_id_type=MESH,
    )
    pieces = ((0, 2 * part), (2 * part, rest))

    def tail_copy(jj):
        piece = pl.ds(*pieces[jj])
        return pltpu.make_async_remote_copy(
            src_ref=tail.at[:, piece], dst_ref=prev.at[:, piece],
            send_sem=tail_send.at[jj], recv_sem=tail_recv.at[jj],
            device_id=to_next, device_id_type=MESH,
        )

    barrier = pltpu.get_barrier_semaphore()
    pl.semaphore_signal(barrier, inc=1, device_id=to_seq, device_id_type=MESH)
    pl.semaphore_signal(barrier, inc=1, device_id=to_sect, device_id_type=MESH)

    @pl.when(inner)
    def _():
        pl.semaphore_signal(barrier, inc=1, device_id=to_cross, device_id_type=MESH)

    @pl.when(has_next)
    def _():
        pl.semaphore_signal(barrier, inc=1, device_id=to_next, device_id_type=MESH)

    @pl.when(has_prev)
    def _():
        pl.semaphore_signal(
            barrier, inc=1, device_id={"span": jnp.maximum(c - 1, 0)}, device_id_type=MESH
        )

    neighbours = 2 + sum(jnp.where(x, 1, 0) for x in (inner, has_next, has_prev))
    pl.semaphore_wait(barrier, neighbours)

    def takes_part(n, cond):
        return cond & inner if n == SHARED else cond

    def straight_near(n):
        @pl.when(takes_part(n, has_next & (q == 1)))
        def _():
            for i in range(2):
                near_copy(n, i, True).start()

    def start_seq(n, i):
        if n == SHARED:
            @pl.when(outer)
            def _():
                seq_copy(n, i).start()

            if i == 0:
                @pl.when(inner)
                def _():
                    lat_copy(0).start()
        else:
            seq_copy(n, i).start()

    def start_own(n):
        for i in range(3):
            own_copy(n, i).start()

    order = [(0, 0), (0, 1)]
    for n in range(SLOTS):
        order += [(n + 1, 0), (n + 1, 1), (n, 2)] if n < LAST else [(n, 2)]
    for item in order[:IN_FLIGHT]:
        start_seq(*item)
    straight_near(0)
    straight_near(1)
    gate_copy.start()
    for n in range(SLOTS):
        if n == SHARED:
            @pl.when(inner)
            def _():
                start_own(SHARED)
                lat_copy(1).start()
        else:
            start_own(n)
    lat_own.start()

    earlier = jnp.maximum(c - 1, 0)
    reach = jnp.where(has_prev, window_ref[earlier], 0)
    first_open = rows - reach * TOK_FRAME
    open_rows = lax.broadcasted_iota(jnp.int32, (rows, HEAD_DIM), 0) >= first_open
    ones = jnp.ones((rows, HEAD_DIM), jnp.bfloat16)
    v_ext[0, :, HEAD_DIM:] = ones
    v_ext[1, :, HEAD_DIM:] = ones
    v_ext[2, :, HEAD_DIM:] = jnp.where(open_rows, 1.0, 0.0).astype(jnp.bfloat16)

    @pl.when(jnp.logical_not(has_prev))
    def _():
        near_k[...] = jnp.zeros_like(near_k)
        near_v[...] = jnp.zeros_like(near_v)
        prev[...] = jnp.zeros_like(prev)

    factor = math.log2(math.e) / math.sqrt(HEAD_DIM)

    def attend(n):
        def one_head(head, carry):
            at = pl.multiple_of(head * HEAD_DIM, HEAD_DIM)
            lanes = pl.ds(at, HEAD_DIM)
            open_now = lax.broadcasted_iota(jnp.int32, (rows, HEAD_DIM), 0) >= first_open
            spare = k_buf[n, 0, :, lanes][:8].astype(jnp.float32)[:1]
            k_mask[...] = jnp.where(
                open_now, near_k[n, :, lanes].astype(jnp.float32), spare
            ).astype(jnp.bfloat16)
            v_ext[0, :, :HEAD_DIM] = v_buf[n, 0, :, lanes]
            v_ext[1, :, :HEAD_DIM] = v_buf[n, 1, :, lanes]
            v_ext[2, :, :HEAD_DIM] = jnp.where(
                open_now, near_v[n, :, lanes].astype(jnp.float32), 0.0
            ).astype(jnp.bfloat16)

            def one_side(who, carry):
                query = q_buf[n, who, :, lanes]
                keys = (k_buf[n, 0, :, lanes], k_buf[n, 1, :, lanes], k_mask[...])
                scores = [
                    lax.dot_general(
                        query, key, (((1,), (1,)), ((), ())), preferred_element_type=jnp.float32
                    )
                    for key in keys
                ]
                top = functools.reduce(
                    jnp.maximum, [jnp.max(x, axis=-1, keepdims=True) for x in scores]
                )
                total = None
                for m, x in enumerate(scores):
                    lifted = jnp.exp2((x - top) * factor).astype(jnp.bfloat16)
                    term = jnp.dot(lifted, v_ext[m], preferred_element_type=jnp.float32)
                    total = term if total is None else total + term
                result = (total[:, :HEAD_DIM] / total[:, HEAD_DIM:]).astype(jnp.bfloat16)
                side = lax.rem(who + q, 2)
                if n <= SHARED:
                    att_far[n, side, :, lanes] = result
                else:
                    here = pl.multiple_of((n - 3) * part + at, HEAD_DIM)
                    att_own[side, :, pl.ds(here, HEAD_DIM)] = result
                return carry

            return lax.fori_loop(0, 2, one_side, carry)

        lax.fori_loop(0, breadth(n) // HEAD_DIM, one_head, 0)

    def finish(jj):
        def block(step, carry):
            at = pl.multiple_of(pieces[jj][0] + step * HEAD_DIM, HEAD_DIM)
            lanes = pl.ds(at, HEAD_DIM)
            spot = pl.ds(pl.multiple_of((2 * s + q) * quarter + at, HEAD_DIM), HEAD_DIM)
            gate_own, gate_other = gate_ref[:, spot], gate_recv[:, spot]
            for side in range(2):
                gated_own = gate_own * att_own[side, :, lanes].astype(jnp.float32)
                gated_other = gate_other * att_recv[side, :, lanes].astype(jnp.float32)
                first = jnp.where(s == 0, gated_own, gated_other)
                later = jnp.where(s == 0, gated_other, gated_own)
                base = lat[lax.rem(side + q, 2), :, lanes].astype(jnp.float32)
                after_one = (base + first).astype(jnp.bfloat16)
                result = after_one.astype(jnp.float32) + later
                second[side, :, lanes] = result.astype(jnp.bfloat16)
                if side == 1:
                    tail[:, lanes] = result[rows - tail_rows:].astype(jnp.bfloat16)
            return carry

        lax.fori_loop(0, pieces[jj][1] // HEAD_DIM, block, 0)

        @pl.when(has_next)
        def _():
            tail_copy(jj).start()

    def ready(n):
        for i in range(3):
            own_copy(n, i).wait()

        @pl.when(has_prev)
        def _():
            for i in range(2):
                near_copy(n, i, False).wait_recv()

        attend(n)

    def arrive(n, i):
        if n == SHARED:
            @pl.when(inner)
            def _():
                seq_copy(n, i).wait_recv()

            @pl.when(outer)
            def _():
                seq_copy(n, i).wait_send()
        else:
            seq_copy(n, i).wait_recv()
        following = order.index((n, i)) + IN_FLIGHT
        if following < len(order):
            start_seq(*order[following])
        if i < 2:
            @pl.when(takes_part(n, has_next & (q == 0)))
            def _():
                near_copy(n, i, False).start()

    for n in range(SLOTS):
        if n == 0:
            arrive(0, 0)
            arrive(0, 1)
        if n < LAST:
            arrive(n + 1, 0)
            arrive(n + 1, 1)
        if n < LAST - 1:
            straight_near(n + 2)
        arrive(n, 2)
        if n == SHARED:
            @pl.when(inner)
            def _():
                ready(SHARED)
                for cross in range(2):
                    shared_copy(cross).start()
        else:
            ready(n)
        if n < SHARED:
            sect_copy(n).start()
        if n == LAST - 1:
            gate_copy.wait_recv()
            lat_own.wait()
            lat_copy(0).wait_recv()
            for m in range(SHARED):
                sect_copy(m).wait_recv()
            shared_copy(0).wait_recv()
            finish(0)
    finish(1)
    for jj in range(2):
        @pl.when(has_prev)
        def _():
            tail_copy(jj).wait_recv()

    @pl.when(inner)
    def _():
        for cross in range(2):
            shared_copy(cross).wait_send()
            lat_copy(cross).wait_send()

    for n in range(SHARED):
        sect_copy(n).wait_send()
    gate_copy.wait_send()
    for n in range(SLOTS):
        if n != SHARED:
            for i in range(3):
                seq_copy(n, i).wait_send()

        @pl.when(takes_part(n, has_next))
        def _():
            for i in range(2):
                near_copy(n, i, False).wait_send()

    @pl.when(has_next)
    def _():
        for jj in range(2):
            tail_copy(jj).wait_send()


def blend_kernel(second, prev, inter_ref, blend_ref, out):
    c = lax.axis_index("span")
    earlier = jnp.maximum(c - 1, 0)
    length = jnp.where(c > 0, inter_ref[earlier], 0)
    out[...] = second[...]

    def frame(f, carry):
        source = pl.ds(pl.multiple_of((BF - length + f) * TOK_FRAME, 16), TOK_FRAME)
        here = pl.ds(pl.multiple_of(f * TOK_FRAME, 16), TOK_FRAME)
        weight = (blend_ref[earlier, f].astype(jnp.float32) + 0.5) / WEIGHTS
        leading = second[0, here, :].astype(jnp.float32)
        mixed = weight * leading + (1.0 - weight) * prev[source, :].astype(jnp.float32)
        out[0, here, :] = mixed.astype(jnp.bfloat16)
        return carry

    lax.fori_loop(0, length, frame, 0)


def local(
    latents, queries, key_states, value_states, gate_scales, window, intersection, blend_index
):
    rows, width = latents.shape
    quarter = width // 4
    part = quarter // HEAD_DIM * 2 // 5 * HEAD_DIM
    spans = lax.axis_size("span")
    tail_rows = BF * TOK_FRAME
    wide = jnp.bfloat16
    dma = pltpu.SemaphoreType.DMA
    flops = 4 * 2 * rows * 3 * rows * width // 2
    smem = pl.BlockSpec(memory_space=pltpu.SMEM)
    vmem = pl.BlockSpec(memory_space=pltpu.VMEM)
    second, prev = pl.pallas_call(
        functools.partial(kernel, spans),
        out_shape=(
            jax.ShapeDtypeStruct((2, rows, quarter), wide),
            jax.ShapeDtypeStruct((tail_rows, quarter), wide),
        ),
        in_specs=[pl.BlockSpec(memory_space=pl.ANY)] * 4 + [vmem, smem],
        out_specs=(vmem, vmem),
        scratch_shapes=[
            pltpu.VMEM((SLOTS, 2, rows, part), wide),
            pltpu.VMEM((SLOTS, 2, rows, part), wide),
            pltpu.VMEM((SLOTS, 2, rows, part), wide),
            pltpu.VMEM((SLOTS, rows, part), wide),
            pltpu.VMEM((SLOTS, rows, part), wide),
            pltpu.VMEM((SHARED + 1, 2, rows, part), wide),
            pltpu.VMEM((2, rows, quarter), wide),
            pltpu.VMEM((2, rows, quarter), wide),
            pltpu.VMEM((2, rows, quarter), wide),
            pltpu.VMEM((tail_rows, quarter), wide),
            pltpu.VMEM(gate_scales.shape, jnp.float32),
            pltpu.VMEM((3, rows, 2 * HEAD_DIM), wide),
            pltpu.VMEM((rows, HEAD_DIM), wide),
            dma((SLOTS, 3)), dma((1,)), dma((SLOTS, 3)), dma((SLOTS, 3)),
            dma((2,)), dma((1,)), dma((SLOTS, 2)), dma((SLOTS, 2)),
            dma((SHARED + 2,)), dma((SHARED + 1,)), dma((1,)), dma((1,)), dma((2,)), dma((2,)),
        ],
        cost_estimate=pl.CostEstimate(
            flops=flops, bytes_accessed=8 * rows * width, transcendentals=flops // 512
        ),
        compiler_params=pltpu.CompilerParams(
            collective_id=0, has_side_effects=True, vmem_limit_bytes=60 * 1024 * 1024
        ),
    )(latents, queries, key_states, value_states, gate_scales, window)
    block = 2 * HEAD_DIM
    result = pl.pallas_call(
        blend_kernel,
        grid=(quarter // block,),
        out_shape=jax.ShapeDtypeStruct((2, rows, quarter), wide),
        in_specs=[
            pl.BlockSpec((2, rows, block), lambda i: (0, 0, i)),
            pl.BlockSpec((tail_rows, block), lambda i: (0, i)),
            smem,
            smem,
        ],
        out_specs=pl.BlockSpec((2, rows, block), lambda i: (0, 0, i)),
        compiler_params=pltpu.CompilerParams(vmem_limit_bytes=60 * 1024 * 1024),
    )(second, prev, intersection, blend_index)
    return result.reshape(2 * rows, quarter)


def solution(mesh):
    in_specs = (
        P(("span", "seq"), None),
        P("section", ("span", "seq"), None),
        P("section", ("span", "seq"), None),
        P("section", ("span", "seq"), None),
        P("section", None),
        P(),
        P(),
        P(),
    )
    out_specs = P("span", ("section", "seq"))
    return jax.shard_map(local, mesh=mesh, in_specs=in_specs, out_specs=out_specs, check_vma=False)
```
